512 devices in a mesh: gx: 16 (over x, z_lo), gy: 32 (over y, z_hi, core).
Axes of the slice: x: 4, y: 4, z: 16 (z_hi: 4, z_lo: 4; z = z_hi * 4 + z_lo), core: 2. Of those that a mesh axis runs over, the one named last changes fastest.
Arguments:
- populations: float32 [19, 2, 128, 4096], P(None, None, 'gx', 'gy'), may hold values from 0.3 to 2.3, as said below
- labels: int32 [2, 128, 4096], P(None, 'gx', 'gy'), may hold values 0 or 1
- solid: int32 [2, 128, 4096], P(None, 'gx', 'gy'), may hold values 0 or 1
- rates: float32 [15], replicated, may hold values from 0.7 to 1.8
Outputs:
- final_state: float32 [2, 19, 2, 128, 4096], P(None, None, None, 'gx', 'gy')
The draws below stay inside these ranges and needn't reach their ends.
Inputs may be any that keep to these rules, and one draw needn't show every extreme that they name: `populations`: each value is a population divided by its lattice weight, near equilibrium with a velocity of at most 0.05 a component and a density between 0.7 and 1.3, with a relative roughness of up to 0.3 a population.
All inputs are finite; a program needn't handle non-finite values. No bound on the sum of `labels` or of `solid` on one device may be relied on, other than what follows from the above.
Results may differ from the reference program's by a relative error of at most 0.0001.
Values sent between devices are 32-bit elements; how exact they have to be, the bound alone decides.
A program may use at most 64 MiB of HBM per device.

```python
import jax
import jax.numpy as jnp
import numpy as np
from jax import lax

DEPTH = 2
ITERS = 6
NX = 128
NY = 4096


velocity_table = np.array([[0, 0, 0], [1, 0, 0], [-1, 0, 0], [0, 1, 0], [0, -1, 0], [0, 0, 1], [0, 0, -1], [1, 1, 0], [-1, -1, 0], [1, -1, 0], [-1, 1, 0], [1, 0, 1], [-1, 0, -1], [1, 0, -1], [-1, 0, 1], [0, 1, 1], [0, -1, -1], [0, 1, -1], [0, -1, 1]])


def draw_populations(key, part):
    subkeys = jax.random.split(jax.random.fold_in(key, 17), 3)
    cell_shape = (DEPTH, NX, NY)
    density = jax.random.uniform(subkeys[0], cell_shape, jnp.float32, 0.7, 1.3)
    roughness = jax.random.uniform(subkeys[2], (19,) + cell_shape, jnp.float32, -0.3, 0.3)
    velocity_field = jax.random.uniform(subkeys[1], (3,) + cell_shape, jnp.float32, -0.05, 0.05)
    velocity = jnp.asarray(velocity_table, jnp.float32)
    projected = jnp.einsum('qd,dxyz->qxyz', velocity, velocity_field)
    squared_speed = jnp.sum(velocity_field * velocity_field, axis=0)
    balance = density[None] * (1.0 + 3.0 * projected + 4.5 * projected * projected - 1.5 * squared_speed[None])
    return (balance * (1.0 + roughness)).astype(jnp.float32)


def set_ends(values, rng, low, largest):
    spot = [jax.random.randint(jax.random.fold_in(rng, axis), (), 0, length) for axis, length in enumerate(values.shape)]
    widest = values.shape.index(max(values.shape))
    next_to = spot[:widest] + [(spot[widest] + 1) % values.shape[widest]] + spot[widest + 1:]
    return values.at[tuple(spot)].set(low).at[tuple(next_to)].set(largest)


def setup_inputs(seed: int = 0) -> dict:
    key_of = jax.random.split(jax.random.key(seed), 5)
    return {
        "populations": draw_populations(jax.random.fold_in(key_of[4], 71), 0),
        "labels": set_ends((jax.random.randint(key_of[1], (DEPTH, NX, NY), 0, 2) < 1).astype(jnp.int32), jax.random.fold_in(key_of[1], 1), 0, 1),
        "solid": set_ends((jax.random.randint(key_of[2], (DEPTH, NX, NY), 0, 4) < 1).astype(jnp.int32), jax.random.fold_in(key_of[2], 1), 0, 1),
        "rates": jnp.clip(jax.random.uniform(key_of[3], (15,), jnp.float32, 0.7, 1.8), 0.7, 1.8),
    }


velocity_table = np.array([[0, 0, 0], [1, 0, 0], [-1, 0, 0], [0, 1, 0], [0, -1, 0], [0, 0, 1], [0, 0, -1], [1, 1, 0], [-1, -1, 0], [1, -1, 0], [-1, 1, 0], [1, 0, 1], [-1, 0, -1], [1, 0, -1], [-1, 0, 1], [0, 1, 1], [0, -1, -1], [0, 1, -1], [0, -1, 1]])
weight_table = np.array([1.0 / 3.0] + [1.0 / 18.0] * 6 + [1.0 / 36.0] * 12)
tension = 0.1
recolor_beta = 0.7
gradient_floor = 0.1

def opposite_of(member):
    return int(np.argmax(np.all(velocity_table == -velocity_table[member], axis=1)))

def build_moments():
    float_table = velocity_table * 1.0
    first_axis = float_table[:, 0]
    second_axis = float_table[:, 1]
    depth_axis = float_table[:, 2]
    squared = first_axis ** 2 + second_axis ** 2 + depth_axis ** 2
    higher = 3.0 * squared - 5.0
    cubic = 5.0 * squared - 9.0
    first_diag = 3.0 * first_axis ** 2 - squared
    cross_diag = second_axis ** 2 - depth_axis ** 2
    listed = [squared * 0.0 + 1.0, 19.0 * squared - 30.0, (21.0 * squared ** 2 - 53.0 * squared + 24.0) / 2.0, first_axis, cubic * first_axis, second_axis, cubic * second_axis, depth_axis, cubic * depth_axis, first_diag, higher * first_diag, cross_diag, higher * cross_diag, first_axis * second_axis, second_axis * depth_axis, first_axis * depth_axis, cross_diag * first_axis, (depth_axis ** 2 - first_axis ** 2) * second_axis, (first_axis ** 2 - second_axis ** 2) * depth_axis]
    return np.array(listed)

def build_placement():
    free_rows = [1, 2, 4, 6, 8] + list(range(9, 19))
    return np.eye(19)[free_rows]

def build_signs():
    return np.array([-1.0] + [1.0] * 18)

def build_lengths():
    return np.maximum(np.sqrt(np.sum((velocity_table * 1.0) ** 2, axis=1)), 1.0)

def lattice_tables():
    velocity = jnp.asarray(velocity_table, jnp.float32)
    weights = jnp.asarray(weight_table, jnp.float32)
    return (velocity, weights)

def relax_matrix(rates):
    moment_table = build_moments()
    inverse_table = moment_table.T / np.sum(moment_table ** 2, axis=1)[None, :]
    relaxation = jnp.dot(rates, jnp.asarray(build_placement(), jnp.float32), precision=lax.Precision.HIGHEST)
    inverse = jnp.asarray(inverse_table, jnp.float32)
    moment = jnp.asarray(moment_table, jnp.float32)
    matrix = jnp.dot(inverse * relaxation[None, :], moment, precision=lax.Precision.HIGHEST)
    weights = jnp.asarray(weight_table, jnp.float32)
    return matrix * weights[None, :] / weights[:, None]

def macroscopic(flattened):
    velocity, weights = lattice_tables()
    moment_rows = jnp.concatenate([weights[None, :], (velocity * weights[:, None]).T], axis=0)
    moments = jnp.dot(moment_rows, flattened[0], precision=lax.Precision.HIGHEST)
    red_mass = jnp.dot(weights[None, :], flattened[1], precision=lax.Precision.HIGHEST)
    return (moments, red_mass)

def collide(flattened, moments, red_mass, gradient, scaled):
    velocity, weights = lattice_tables()
    density = moments[0:1]
    velocity_field = moments[1:4] / density
    projected = jnp.dot(velocity, velocity_field, precision=lax.Precision.HIGHEST)
    squared_speed = lax.optimization_barrier(jnp.sum(velocity_field * velocity_field, axis=0, keepdims=True))
    balance = density * (1.0 + 3.0 * projected + 4.5 * projected * projected - 1.5 * squared_speed)
    relaxed = flattened[0] - jnp.dot(scaled, flattened[0] - balance, precision=lax.Precision.HIGHEST)
    magnitude = jnp.sqrt(lax.optimization_barrier(jnp.sum(gradient * gradient, axis=0, keepdims=True)))
    bounded = jnp.maximum(magnitude, gradient_floor)
    aligned = jnp.dot(velocity, gradient, precision=lax.Precision.HIGHEST)
    sign_column = jnp.asarray(build_signs(), jnp.float32)[:, None]
    relaxed = relaxed + 0.5 * tension * (aligned * aligned / bounded - sign_column * magnitude)
    lengths = jnp.asarray(build_lengths(), jnp.float32)[:, None]
    fraction = red_mass / density
    mixing = recolor_beta * red_mass * (density - red_mass) / density
    recolored = fraction * relaxed + mixing * aligned / (lengths * bounded)
    return jnp.stack([relaxed, recolored])

def gradient_whole(phase_field):
    components = [jnp.zeros(phase_field.shape, jnp.float32) for axis_number in range(3)]
    for member in range(1, 19):
        along_first, along_second, along_depth = (int(value) for value in velocity_table[member])
        shifted = jnp.roll(phase_field, (-along_depth, -along_first, -along_second), axis=(0, 1, 2))
        factor = 3.0 * float(weight_table[member])
        for axis_number, along in enumerate((along_first, along_second, along_depth)):
            if along != 0:
                components[axis_number] = components[axis_number] + factor * along * shifted
    return jnp.stack(components)

def stream_whole(collided, current, blocked):
    results = []
    for member in range(19):
        along_first, along_second, along_depth = (int(value) for value in velocity_table[member])
        shifted = jnp.roll(collided[:, member], (along_depth, along_first, along_second), axis=(1, 2, 3))
        source_rock = jnp.roll(blocked, (along_depth, along_first, along_second), axis=(0, 1, 2))
        bounced = collided[:, opposite_of(member)]
        pulled = jnp.where(source_rock[None], bounced, shifted)
        results.append(jnp.where(blocked[None], current[:, member], pulled))
    return jnp.stack(results, axis=1)

def reference(populations, labels, solid, rates):
    scaled = relax_matrix(rates)
    red_part = labels.astype(jnp.float32)[None] * populations
    current = jnp.stack([populations, red_part])
    blocked = solid > 0
    grid_shape = current.shape
    for iteration in range(ITERS):
        flattened = current.reshape(2, 19, -1)
        moments, red_mass = macroscopic(flattened)
        phase_field = ((2.0 * red_mass - moments[0:1]) / moments[0:1]).reshape(grid_shape[2:])
        gradient = gradient_whole(phase_field).reshape(3, -1)
        collided = collide(flattened, moments, red_mass, gradient, scaled).reshape(grid_shape)
        current = stream_whole(collided, current, blocked)
    return current
```

```python
import functools

import jax
import jax.numpy as jnp
import numpy as np
from jax import lax
from jax.experimental import pallas as pl
from jax.experimental.pallas import tpu as pltpu
from jax.sharding import PartitionSpec as P

ITERS = 6
HALO = 2 * ITERS
MESH = pl.DeviceIdType.MESH

velocity_table = np.array(
    [
        [0, 0, 0],
        [1, 0, 0],
        [-1, 0, 0],
        [0, 1, 0],
        [0, -1, 0],
        [0, 0, 1],
        [0, 0, -1],
        [1, 1, 0],
        [-1, -1, 0],
        [1, -1, 0],
        [-1, 1, 0],
        [1, 0, 1],
        [-1, 0, -1],
        [1, 0, -1],
        [-1, 0, 1],
        [0, 1, 1],
        [0, -1, -1],
        [0, 1, -1],
        [0, -1, 1],
    ]
)
half_tension = 0.05
recolor_beta = 0.7
gradient_floor = 0.1
ROWS = 8
LANES = 128
EXTENT = ROWS + 2 * HALO
CHUNK = 16
PER_PLANE = LANES // CHUNK
PLANES = 42
PACKED = -(-PLANES // PER_PLANE)


def opposite_of(member):
    return int(np.argmax(np.all(velocity_table == -velocity_table[member], axis=1)))


OPPOSITE = [opposite_of(member) for member in range(19)]


def placement(dx):
    first = HALO - ROWS * dx
    low, high = max(first, 0), min(first + ROWS, EXTENT)
    return low - first, low, high - low


def gather_kernel(pop_hbm, flag_hbm, ext_ref, flags_ref, strip_ref, pop, flag, right, left, send, recv, local):
    gx, gy = lax.axis_index("gx"), lax.axis_index("gy")
    nx, ny = lax.axis_size("gx"), lax.axis_size("gy")
    offsets = [(dx, dy) for dy in (1, -1) for dx in (1, -1, 0, 2, -2)] + [(1, 0), (-1, 0), (2, 0), (-2, 0)]
    device = {
        (dx, dy): (lax.rem(gx + (dx + nx), nx), lax.rem(gy + (dy + ny), ny)) for dx, dy in offsets
    }
    barrier = pltpu.get_barrier_semaphore()
    for offset in offsets:
        pl.semaphore_signal(barrier, inc=1, device_id=device[offset], device_id_type=MESH)
    loads = [
        pltpu.make_async_copy(pop_hbm, pop, local.at[0]),
        pltpu.make_async_copy(flag_hbm, flag, local.at[1]),
    ]
    for copy in loads:
        copy.start()
    for copy in loads:
        copy.wait()
    keep = [
        pltpu.make_async_copy(pop, ext_ref.at[:, :, HALO : HALO + ROWS, :], local.at[2]),
        pltpu.make_async_copy(flag, flags_ref.at[:, :, HALO : HALO + ROWS, :], local.at[3]),
    ]
    for copy in keep:
        copy.start()

    chunk = lax.broadcasted_iota(jnp.int32, (ROWS, LANES), 1) // CHUNK
    for first in range(0, PLANES, PER_PLANE):
        to_left = to_right = None
        for slot in range(min(PER_PLANE, PLANES - first)):
            plane = first + slot
            value = pop[plane // 2, plane % 2] if plane < 38 else flag[(plane - 38) // 2, plane % 2]
            moved = value if slot == 0 else pltpu.roll(value, CHUNK * slot, 1)
            to_left = moved if slot == 0 else jnp.where(chunk == slot, moved, to_left)
            before = (slot - 1) % PER_PLANE
            to_right = moved if slot == 0 else jnp.where(chunk == before, moved, to_right)
        left[first // PER_PLANE] = to_left
        right[first // PER_PLANE] = to_right

    pl.semaphore_wait(barrier, len(offsets))
    copies = []

    def push(source, target, device_id):
        number = len(copies)
        copy = pltpu.make_async_remote_copy(
            src_ref=source,
            dst_ref=target,
            send_sem=send.at[number],
            recv_sem=recv.at[number],
            device_id=device_id,
            device_id_type=MESH,
        )
        copy.start()
        copies.append(copy)

    for dx, dy in offsets:
        begin, low, count = placement(dx)
        if dy != 0:
            source = right if dy > 0 else left
            push(
                source.at[:, begin : begin + count, :],
                strip_ref.at[0 if dy > 0 else 1, :, low : low + count, :],
                device[dx, dy],
            )
            continue
        push(
            flag.at[:, :, begin : begin + count, :],
            flags_ref.at[:, :, low : low + count, :],
            device[dx, dy],
        )
        if dx == 2:
            begin, low, count = begin + 1, low + 1, count - 1
        if dx == -2:
            count = count - 1
        push(
            pop.at[:, :, begin : begin + count, :],
            ext_ref.at[:, :, low : low + count, :],
            device[dx, dy],
        )
    for copy in keep:
        copy.wait()
    for copy in copies:
        copy.wait_recv()
    for copy in copies:
        copy.wait_send()


def gather(populations, flags):
    shapes = [
        jax.ShapeDtypeStruct((19, 2, EXTENT, LANES), jnp.float32),
        jax.ShapeDtypeStruct((2, 2, EXTENT, LANES), jnp.float32),
        jax.ShapeDtypeStruct((2, PACKED, EXTENT, LANES), jnp.float32),
    ]
    anywhere = pl.BlockSpec(memory_space=pl.ANY)
    return pl.pallas_call(
        gather_kernel,
        out_shape=shapes,
        in_specs=[anywhere] * 2,
        out_specs=[anywhere] * 3,
        scratch_shapes=[
            pltpu.VMEM((19, 2, ROWS, LANES), jnp.float32),
            pltpu.VMEM((2, 2, ROWS, LANES), jnp.float32),
            pltpu.VMEM((PACKED, ROWS, LANES), jnp.float32),
            pltpu.VMEM((PACKED, ROWS, LANES), jnp.float32),
            pltpu.SemaphoreType.DMA((18,)),
            pltpu.SemaphoreType.DMA((18,)),
            pltpu.SemaphoreType.DMA((4,)),
        ],
        compiler_params=pltpu.CompilerParams(collective_id=0, has_side_effects=True),
    )(populations, flags)


def lateral(pair, dy, lane):
    if dy == 0:
        return pair
    edge = lane == (LANES - 1 if dy > 0 else 0)
    return [
        pltpu.roll(jnp.where(edge, pair[1 - part], pair[part]), dy % LANES, 1) for part in range(2)
    ]


def relax(f, rate):
    plus = {q: f[q] + f[q + 1] for q in range(1, 19, 2)}
    minus = {q: f[q] - f[q + 1] for q in range(1, 19, 2)}
    both = {q: plus[q] + plus[q + 2] for q in (7, 11, 15)}
    cross = {q: plus[q] - plus[q + 2] for q in (7, 11, 15)}
    head = {q: minus[q] + minus[q + 2] for q in (7, 11, 15)}
    tail = {q: minus[q] - minus[q + 2] for q in (7, 11, 15)}
    axes = plus[1] + plus[3] + plus[5]
    diagonals = both[7] + both[11] + both[15]
    density = f[0] * (1.0 / 3.0) + axes * (1.0 / 18.0) + diagonals * (1.0 / 36.0)
    momentum = [
        minus[1] * (1.0 / 18.0) + (head[7] + head[11]) * (1.0 / 36.0),
        minus[3] * (1.0 / 18.0) + (tail[7] + head[15]) * (1.0 / 36.0),
        minus[5] * (1.0 / 18.0) + (tail[11] + tail[15]) * (1.0 / 36.0),
    ]
    inverse = 1.0 / density
    speed = [part * inverse for part in momentum]
    xx, yy, zz = (momentum[k] * speed[k] for k in range(3))
    xy, yz, xz = momentum[0] * speed[1], momentum[1] * speed[2], momentum[0] * speed[2]
    square = xx + yy + zz
    energy = f[0] * -10.0 + axes * (-11.0 / 18.0) + diagonals * (8.0 / 36.0) - (19.0 * square - 11.0 * density)
    fourth = f[0] * 4.0 + axes * (-4.0 / 18.0) + diagonals * (1.0 / 36.0) - (3.0 * density - 5.5 * square)
    first_axis = (3.0 * plus[1] - axes) * (1.0 / 18.0)
    first_diag = (diagonals - 3.0 * both[15]) * (1.0 / 36.0)
    first_flow = 3.0 * xx - square
    second_axis = (plus[3] - plus[5]) * (1.0 / 18.0)
    second_diag = (both[7] - both[11]) * (1.0 / 36.0)
    second_flow = yy - zz
    energy = energy * (rate[0] * (1.0 / 2394.0))
    fourth = fourth * (rate[1] * (1.0 / 252.0))
    first = (first_axis + first_diag - first_flow) * (rate[5] * (1.0 / 36.0))
    first_high = (first_diag - 2.0 * first_axis + 0.5 * first_flow) * (rate[6] * (1.0 / 72.0))
    second = (second_axis + second_diag - second_flow) * (rate[7] * (1.0 / 12.0))
    second_high = (second_diag - 2.0 * second_axis + 0.5 * second_flow) * (rate[8] * (1.0 / 24.0))
    on_rest = energy * -90.0 + fourth * 36.0
    on_axes = energy * -198.0 - fourth * 72.0
    on_diagonals = energy * 288.0 + fourth * 36.0
    axis_first = (first - 2.0 * first_high) * 18.0
    axis_second = (second - 2.0 * second_high) * 18.0
    diag_first = (first + first_high) * 36.0
    diag_second = (second + second_high) * 36.0
    rest_axes = on_axes - axis_first
    along = [on_axes + 2.0 * axis_first, rest_axes + axis_second, rest_axes - axis_second]
    near = on_diagonals + diag_first
    around = {7: near + diag_second, 11: near - diag_second, 15: on_diagonals - 2.0 * diag_first}
    shear = {
        7: (cross[7] * (1.0 / 36.0) - xy) * (rate[9] * 9.0),
        15: (cross[15] * (1.0 / 36.0) - yz) * (rate[10] * 9.0),
        11: (cross[11] * (1.0 / 36.0) - xz) * (rate[11] * 9.0),
    }
    flux = []
    for k, diag in enumerate((head[7] + head[11], tail[7] + head[15], tail[11] + tail[15])):
        moment = minus[2 * k + 1] * (-4.0 / 18.0) + diag * (1.0 / 36.0) + momentum[k] * (2.0 / 3.0)
        flux.append(moment * (rate[2 + k] * 0.9))
    twist = [
        (head[7] - head[11]) * (rate[12] * (4.5 / 36.0)),
        (head[15] - tail[7]) * (rate[13] * (4.5 / 36.0)),
        (tail[11] - tail[15]) * (rate[14] * (4.5 / 36.0)),
    ]
    left = [None] * 19
    left[0] = f[0] - on_rest
    for k in range(3):
        double = 2.0 * flux[k]
        left[2 * k + 1] = f[2 * k + 1] - (along[k] - double)
        left[2 * k + 2] = f[2 * k + 2] - (along[k] + double)
    odd = {
        7: (flux[0] + twist[0], flux[1] - twist[1]),
        11: (flux[0] - twist[0], flux[2] + twist[2]),
        15: (flux[1] + twist[1], flux[2] - twist[2]),
    }
    for q in (7, 11, 15):
        same, other = around[q] + shear[q], around[q] - shear[q]
        total, gap = odd[q][0] + odd[q][1], odd[q][0] - odd[q][1]
        left[q] = f[q] - (same + total)
        left[q + 1] = f[q + 1] - (same - total)
        left[q + 2] = f[q + 2] - (other + gap)
        left[q + 3] = f[q + 3] - (other - gap)
    return density, inverse, left


def weighted_sum(f):
    axes = functools.reduce(lambda a, b: a + b, f[1:7])
    diagonals = functools.reduce(lambda a, b: a + b, f[7:19])
    return f[0] * (1.0 / 3.0) + axes * (1.0 / 18.0) + diagonals * (1.0 / 36.0)


def windows(low, high):
    count = -(-(high - low) // ROWS)
    return count, high - ROWS


def steps_kernel(rate_ref, ext, flags, strips, out, left_ref, frac_ref, mix_ref, total_ref, red_ref, label_ref, rock_ref):
    rate = [rate_ref[k] for k in range(15)]
    lane = lax.broadcasted_iota(jnp.int32, (ROWS, LANES), 1)
    right_half = lane < LANES // 2

    def rows_of(index, low, high):
        return jnp.minimum(low + ROWS * index, high - ROWS)

    def keep(d, part, rows, density, share, remains):
        frac_ref[d, part, rows, :] = share
        mix_ref[d, part, rows, :] = recolor_beta * density * share * (1.0 - share)
        for q in range(19):
            left_ref[q, d, part, rows, :] = remains[q]

    def start(index, carry):
        w, d = index // 2, lax.rem(index, 2)
        rows = pl.ds(pl.multiple_of(w * ROWS, ROWS), ROWS)

        def strip(plane):
            first, second = [], []
            for depth in range(2):
                number = 2 * plane + depth
                which, slot = number // PER_PLANE, number % PER_PLANE
                moved = [strips[side, which, rows, :] for side in range(2)]
                if slot:
                    moved = [pltpu.roll(value, LANES - CHUNK * slot, 1) for value in moved]
                first.append(jnp.where(right_half, moved[1], moved[0]))
            return jnp.where(d == 0, first[0], first[1])

        label = [flags[0, d, rows, :], strip(19)]
        rock = [flags[1, d, rows, :], strip(20)]
        for dy in (-1, 0, 1):
            moved = lateral(rock, dy, lane)
            for part in range(2):
                rock_ref[dy + 1, d, part, rows, :] = moved[part]
        for part in range(2):
            label_ref[d, part, rows, :] = label[part]
        f = [[ext[q, d, rows, :] for q in range(19)], [strip(q) for q in range(19)]]
        for part in range(2):
            density, _, remains = relax(f[part], rate)
            keep(d, part, rows, density, label[part], remains)
        return carry

    lax.fori_loop(0, 2 * (EXTENT // ROWS), start, 0)

    def collide(low, high, index, carry):
        w, d = index // 2, lax.rem(index, 2)
        row = rows_of(w, low, high)
        here = pl.ds(row, ROWS)
        mine, theirs = {}, {}
        for dx in (-1, 0, 1):
            rows = pl.ds(row + dx, ROWS)
            mine[dx] = [frac_ref[d, part, rows, :] for part in range(2)]
            theirs[dx] = [frac_ref[1 - d, part, rows, :] for part in range(2)]
        planes = {dx: [(mine[dx][k] + theirs[dx][k]) * (1.0 / 3.0) for k in range(2)] for dx in (-1, 0, 1)}
        slope = [(mine[1][k] - mine[-1][k]) * (1.0 / 6.0) for k in range(2)]
        ahead, behind = lateral(slope, -1, lane), lateral(slope, 1, lane)
        level = [planes[0][k] + (mine[1][k] + mine[-1][k]) * (1.0 / 6.0) for k in range(2)]
        after, before = lateral(level, -1, lane), lateral(level, 1, lane)
        for part in range(2):
            gx = planes[1][part] - planes[-1][part] + ahead[part] + behind[part]
            gy = after[part] - before[part]
            both, gap = gx + gy, gx - gy
            magnitude = jnp.sqrt(gx * gx + gy * gy)
            inverse = 1.0 / jnp.maximum(magnitude, gradient_floor)
            pull = half_tension * magnitude
            scale = half_tension * inverse
            added = {
                (0, 0): -pull,
                (1, 0): gx * gx * scale - pull,
                (0, 1): gy * gy * scale - pull,
                (1, 1): both * both * scale - pull,
                (1, -1): gap * gap * scale - pull,
            }
            share = mine[0][part]
            mixing = mix_ref[d, part, here, :] * inverse
            diagonal = mixing * float(1.0 / np.sqrt(2.0))
            turned = {
                (1, 0, 0): mixing * gx,
                (0, 1, 0): mixing * gy,
                (1, 1, 0): diagonal * both,
                (1, -1, 0): diagonal * gap,
                (1, 0, 1): diagonal * gx,
                (0, 1, 1): diagonal * gy,
            }
            for q in range(19):
                a, b, c = (int(v) for v in velocity_table[q])
                remains = left_ref[q, d, part, here, :]
                sign = 1 if (a, b) > (0, 0) else -1
                key = (a * sign, b * sign) if (a, b) != (0, 0) else (0, 0)
                value = remains + pull if q == 0 else remains + added[key]
                total_ref[q, d, part, here, :] = value
                red = share * value
                if key != (0, 0):
                    turn = turned[key[0], key[1], abs(c)]
                    red = red + turn if sign > 0 else red - turn
                red_ref[q, d, part, here, :] = red
        return carry

    def stream(row, d, parts):
        here = pl.ds(row, ROWS)
        totals, reds = [[], []], [[], []]
        for q in range(19):
            a, b, c = (int(v) for v in velocity_table[q])
            rows = pl.ds(row - a, ROWS)
            source = d if c == 0 else 1 - d
            for ref, found in ((total_ref, totals), (red_ref, reds)):
                if b == 0:
                    moved = [ref[q, source, part, rows, :] for part in range(parts)]
                else:
                    pair = [ref[q, source, part, rows, :] for part in range(2)]
                    edge = lane == (LANES - 1 if b > 0 else 0)
                    moved = [
                        pltpu.roll(jnp.where(edge, pair[1 - part], pair[part]), b % LANES, 1)
                        for part in range(parts)
                    ]
                for part in range(parts):
                    value = moved[part]
                    if q:
                        wall = rock_ref[b + 1, source, part, rows, :] > 0.5
                        value = jnp.where(wall, ref[OPPOSITE[q], d, part, here, :], value)
                    found[part].append(value)
        return totals, reds

    def advance(low, high, index, carry):
        w, d = index // 2, lax.rem(index, 2)
        row = rows_of(w, low, high)
        here = pl.ds(row, ROWS)
        totals, reds = stream(row, d, 2)
        for part in range(2):
            density, inverse, remains = relax(totals[part], rate)
            rock = rock_ref[1, d, part, here, :] > 0.5
            label = label_ref[d, part, here, :]
            share = jnp.where(rock, label, weighted_sum(reds[part]) * inverse)
            keep(d, part, here, density, share, remains)
        return carry

    for step in range(ITERS):
        low, high = 2 * step + 1, EXTENT - 2 * step - 1
        lax.fori_loop(0, 2 * windows(low, high)[0], functools.partial(collide, low, high), 0)
        low, high = low + 1, high - 1
        if step < ITERS - 1:
            lax.fori_loop(0, 2 * windows(low, high)[0], functools.partial(advance, low, high), 0)

    def finish(d, carry):
        totals, reds = stream(HALO, d, 1)
        here = pl.ds(HALO, ROWS)
        rock = rock_ref[1, d, 0, here, :] > 0.5
        label = label_ref[d, 0, here, :]
        for q in range(19):
            first = ext[q, d, here, :]
            out[0, q, d] = jnp.where(rock, first, totals[0][q])
            out[1, q, d] = jnp.where(rock, label * first, reds[0][q])
        return carry

    lax.fori_loop(0, 2, finish, 0)


def steps(rates, ext, flags, strips):
    whole = pl.BlockSpec(memory_space=pltpu.VMEM)
    field = (2, 2, EXTENT, LANES)
    return pl.pallas_call(
        steps_kernel,
        out_shape=jax.ShapeDtypeStruct((2, 19, 2, ROWS, LANES), jnp.float32),
        in_specs=[pl.BlockSpec(memory_space=pltpu.SMEM)] + [whole] * 3,
        out_specs=whole,
        scratch_shapes=[
            pltpu.VMEM((19,) + field, jnp.float32),
            pltpu.VMEM(field, jnp.float32),
            pltpu.VMEM(field, jnp.float32),
            pltpu.VMEM((19,) + field, jnp.float32),
            pltpu.VMEM((19,) + field, jnp.float32),
            pltpu.VMEM(field, jnp.float32),
            pltpu.VMEM((3,) + field, jnp.float32),
        ],
        compiler_params=pltpu.CompilerParams(vmem_limit_bytes=32 * 2**20),
    )(rates, ext, flags, strips)


def body(populations, labels, solid, rates):
    flags = jnp.stack([labels, (solid > 0).astype(labels.dtype)]).astype(jnp.float32)
    ext, flags, strips = gather(populations, flags)
    return steps(rates, ext, flags, strips)


def solution(mesh):
    return jax.shard_map(
        body,
        mesh=mesh,
        in_specs=(P(None, None, "gx", "gy"), P(None, "gx", "gy"), P(None, "gx", "gy"), P()),
        out_specs=P(None, None, None, "gx", "gy"),
        check_vma=False,
    )
```

```python
import functools

import jax
import jax.numpy as jnp
import numpy as np
from jax import lax
from jax.experimental import pallas as pl
from jax.experimental.pallas import tpu as pltpu
from jax.sharding import PartitionSpec as P

ITERS = 6
ROUNDS = 2
STEPS = ITERS // ROUNDS
HALO = 2 * STEPS
MESH = pl.DeviceIdType.MESH

velocity_table = np.array(
    [
        [0, 0, 0],
        [1, 0, 0],
        [-1, 0, 0],
        [0, 1, 0],
        [0, -1, 0],
        [0, 0, 1],
        [0, 0, -1],
        [1, 1, 0],
        [-1, -1, 0],
        [1, -1, 0],
        [-1, 1, 0],
        [1, 0, 1],
        [-1, 0, -1],
        [1, 0, -1],
        [-1, 0, 1],
        [0, 1, 1],
        [0, -1, -1],
        [0, 1, -1],
        [0, -1, 1],
    ]
)
half_tension = 0.05
recolor_beta = 0.7
gradient_floor = 0.1
ROWS = 8
LANES = 128
EXTENT = ROWS + 2 * HALO
CHUNK = 8
PER_STRIP = LANES // CHUNK
FIELDS = 21
PACKED = -(-2 * FIELDS // PER_STRIP)
OWN = slice(HALO, HALO + ROWS)


def opposite_of(member):
    return int(np.argmax(np.all(velocity_table == -velocity_table[member], axis=1)))


OPPOSITE = [opposite_of(member) for member in range(19)]


def placement(dx):
    first = HALO - ROWS * dx
    low, high = max(first, 0), min(first + ROWS, EXTENT)
    return low - first, low, high - low


def lateral(pair, dy, lane):
    if dy == 0:
        return pair
    edge = lane == (LANES - 1 if dy > 0 else 0)
    return [
        pltpu.roll(jnp.where(edge, pair[1 - part], pair[part]), dy % LANES, 1) for part in range(2)
    ]


def relax(f, rate):
    plus = {q: f[q] + f[q + 1] for q in range(1, 19, 2)}
    minus = {q: f[q] - f[q + 1] for q in range(1, 19, 2)}
    both = {q: plus[q] + plus[q + 2] for q in (7, 11, 15)}
    cross = {q: plus[q] - plus[q + 2] for q in (7, 11, 15)}
    head = {q: minus[q] + minus[q + 2] for q in (7, 11, 15)}
    tail = {q: minus[q] - minus[q + 2] for q in (7, 11, 15)}
    axes = plus[1] + plus[3] + plus[5]
    diagonals = both[7] + both[11] + both[15]
    density = f[0] * (1.0 / 3.0) + axes * (1.0 / 18.0) + diagonals * (1.0 / 36.0)
    momentum = [
        minus[1] * (1.0 / 18.0) + (head[7] + head[11]) * (1.0 / 36.0),
        minus[3] * (1.0 / 18.0) + (tail[7] + head[15]) * (1.0 / 36.0),
        minus[5] * (1.0 / 18.0) + (tail[11] + tail[15]) * (1.0 / 36.0),
    ]
    inverse = 1.0 / density
    speed = [part * inverse for part in momentum]
    xx, yy, zz = (momentum[k] * speed[k] for k in range(3))
    xy, yz, xz = momentum[0] * speed[1], momentum[1] * speed[2], momentum[0] * speed[2]
    square = xx + yy + zz
    energy = f[0] * -10.0 + axes * (-11.0 / 18.0) + diagonals * (8.0 / 36.0) - (19.0 * square - 11.0 * density)
    fourth = f[0] * 4.0 + axes * (-4.0 / 18.0) + diagonals * (1.0 / 36.0) - (3.0 * density - 5.5 * square)
    first_axis = (3.0 * plus[1] - axes) * (1.0 / 18.0)
    first_diag = (diagonals - 3.0 * both[15]) * (1.0 / 36.0)
    first_flow = 3.0 * xx - square
    second_axis = (plus[3] - plus[5]) * (1.0 / 18.0)
    second_diag = (both[7] - both[11]) * (1.0 / 36.0)
    second_flow = yy - zz
    energy = energy * (rate[0] * (1.0 / 2394.0))
    fourth = fourth * (rate[1] * (1.0 / 252.0))
    first = (first_axis + first_diag - first_flow) * (rate[5] * (1.0 / 36.0))
    first_high = (first_diag - 2.0 * first_axis + 0.5 * first_flow) * (rate[6] * (1.0 / 72.0))
    second = (second_axis + second_diag - second_flow) * (rate[7] * (1.0 / 12.0))
    second_high = (second_diag - 2.0 * second_axis + 0.5 * second_flow) * (rate[8] * (1.0 / 24.0))
    on_rest = energy * -90.0 + fourth * 36.0
    on_axes = energy * -198.0 - fourth * 72.0
    on_diagonals = energy * 288.0 + fourth * 36.0
    axis_first = (first - 2.0 * first_high) * 18.0
    axis_second = (second - 2.0 * second_high) * 18.0
    diag_first = (first + first_high) * 36.0
    diag_second = (second + second_high) * 36.0
    rest_axes = on_axes - axis_first
    along = [on_axes + 2.0 * axis_first, rest_axes + axis_second, rest_axes - axis_second]
    near = on_diagonals + diag_first
    around = {7: near + diag_second, 11: near - diag_second, 15: on_diagonals - 2.0 * diag_first}
    shear = {
        7: (cross[7] * (1.0 / 36.0) - xy) * (rate[9] * 9.0),
        15: (cross[15] * (1.0 / 36.0) - yz) * (rate[10] * 9.0),
        11: (cross[11] * (1.0 / 36.0) - xz) * (rate[11] * 9.0),
    }
    flux = []
    for k, diag in enumerate((head[7] + head[11], tail[7] + head[15], tail[11] + tail[15])):
        moment = minus[2 * k + 1] * (-4.0 / 18.0) + diag * (1.0 / 36.0) + momentum[k] * (2.0 / 3.0)
        flux.append(moment * (rate[2 + k] * 0.9))
    twist = [
        (head[7] - head[11]) * (rate[12] * (4.5 / 36.0)),
        (head[15] - tail[7]) * (rate[13] * (4.5 / 36.0)),
        (tail[11] - tail[15]) * (rate[14] * (4.5 / 36.0)),
    ]
    left = [None] * 19
    left[0] = f[0] - on_rest
    for k in range(3):
        double = 2.0 * flux[k]
        left[2 * k + 1] = f[2 * k + 1] - (along[k] - double)
        left[2 * k + 2] = f[2 * k + 2] - (along[k] + double)
    odd = {
        7: (flux[0] + twist[0], flux[1] - twist[1]),
        11: (flux[0] - twist[0], flux[2] + twist[2]),
        15: (flux[1] + twist[1], flux[2] - twist[2]),
    }
    for q in (7, 11, 15):
        same, other = around[q] + shear[q], around[q] - shear[q]
        total, gap = odd[q][0] + odd[q][1], odd[q][0] - odd[q][1]
        left[q] = f[q] - (same + total)
        left[q + 1] = f[q + 1] - (same - total)
        left[q + 2] = f[q + 2] - (other + gap)
        left[q + 3] = f[q + 3] - (other - gap)
    return density, inverse, left


def weighted_sum(f):
    axes = functools.reduce(lambda a, b: a + b, f[1:7])
    diagonals = functools.reduce(lambda a, b: a + b, f[7:19])
    return f[0] * (1.0 / 3.0) + axes * (1.0 / 18.0) + diagonals * (1.0 / 36.0)


def over_windows(low, high, work):
    count = -(-(high - low) // ROWS)
    if count == 1:
        work(low)
        return

    def one(index, carry):
        work(jnp.minimum(low + ROWS * index, high - ROWS))
        return carry

    lax.fori_loop(0, count, one, 0)


def kernel(
    rate_ref, pop_hbm, label_hbm, solid_hbm, out, *scratch
):
    states, strips = scratch[:ROUNDS], scratch[ROUNDS : 2 * ROUNDS]
    packs, codes, left_ref, frac_ref, mix_ref, total_ref, red_ref, label_ref, rock_ref, send, recv, local = scratch[2 * ROUNDS :]
    gx, gy = lax.axis_index("gx"), lax.axis_index("gy")
    nx, ny = lax.axis_size("gx"), lax.axis_size("gy")
    offsets = [(dx, dy) for dy in (1, -1) for dx in (1, -1, 0)] + [(1, 0), (-1, 0)]
    device = {
        (dx, dy): (lax.rem(gx + (dx + nx), nx), lax.rem(gy + (dy + ny), ny)) for dx, dy in offsets
    }
    barrier = pltpu.get_barrier_semaphore()
    for offset in offsets:
        pl.semaphore_signal(barrier, inc=1, device_id=device[offset], device_id_type=MESH)
    loads = [
        pltpu.make_async_copy(label_hbm, codes.at[0], local.at[1]),
        pltpu.make_async_copy(solid_hbm, codes.at[1], local.at[2]),
        pltpu.make_async_copy(pop_hbm, states[0].at[0:19, :, OWN, :], local.at[0]),
    ]
    for copy in loads:
        copy.start()
    for copy in loads:
        copy.wait()
    for d in range(2):
        states[0][19, d, OWN, :] = codes[0, d].astype(jnp.float32)
        states[0][20, d, OWN, :] = jnp.where(codes[1, d] > 0, 1.0, 0.0)

    rate = [rate_ref[k] for k in range(15)]
    lane = lax.broadcasted_iota(jnp.int32, (ROWS, LANES), 1)
    chunk = lane // CHUNK
    right_half = lane < LANES // 2

    def pack(number, fields):
        for first in range(0, 2 * fields, PER_STRIP):
            to_left = to_right = None
            for slot in range(min(PER_STRIP, 2 * fields - first)):
                plane = first + slot
                value = states[number][plane // 2, plane % 2, OWN, :]
                moved = value if slot == 0 else pltpu.roll(value, CHUNK * slot, 1)
                to_left = moved if slot == 0 else jnp.where(chunk == slot, moved, to_left)
                before = (slot - 1) % PER_STRIP
                to_right = moved if slot == 0 else jnp.where(chunk == before, moved, to_right)
            packs[number, 0, first // PER_STRIP] = to_right
            packs[number, 1, first // PER_STRIP] = to_left

    def exchange(number, fields):
        copies = []
        for dx, dy in offsets:
            begin, low, count = placement(dx)
            if dy != 0:
                side, used = (0 if dy > 0 else 1), -(-2 * fields // PER_STRIP)
                source = packs.at[number, side, 0:used, begin : begin + count, :]
                target = strips[number].at[side, 0:used, low : low + count, :]
            else:
                source = states[number].at[0:fields, :, HALO + begin : HALO + begin + count, :]
                target = states[number].at[0:fields, :, low : low + count, :]
            place = len(copies)
            copy = pltpu.make_async_remote_copy(
                src_ref=source,
                dst_ref=target,
                send_sem=send.at[number, place],
                recv_sem=recv.at[number, place],
                device_id=device[dx, dy],
                device_id_type=MESH,
            )
            copy.start()
            copies.append(copy)
        for copy in copies:
            copy.wait_recv()
        return copies

    def strip(number, field, d, rows):
        plane = 2 * field + d
        which, slot = plane // PER_STRIP, plane % PER_STRIP
        moved = [strips[number][side, which, rows, :] for side in range(2)]
        if slot:
            moved = [pltpu.roll(value, LANES - CHUNK * slot, 1) for value in moved]
        return jnp.where(right_half, moved[1], moved[0])

    def keep(d, part, rows, density, share, remains):
        frac_ref[d, part, rows, :] = share
        mix_ref[d, part, rows, :] = recolor_beta * density * share * (1.0 - share)
        for q in range(19):
            left_ref[q, d, part, rows, :] = remains[q]

    def start(number, row):
        rows = pl.ds(row, ROWS)
        for d in range(2):

            def both_of(field):
                return [states[number][field, d, rows, :], strip(number, field, d, rows)]

            share = both_of(19)
            if number == 0:
                rock = both_of(20)
                for dy in (-1, 0, 1):
                    moved = lateral(rock, dy, lane)
                    for part in range(2):
                        rock_ref[dy + 1, d, part, rows, :] = moved[part]
                for part in range(2):
                    label_ref[d, part, rows, :] = share[part]
            f = [both_of(q) for q in range(19)]
            for part in range(2):
                density, _, remains = relax([pair[part] for pair in f], rate)
                keep(d, part, rows, density, share[part], remains)

    def collide(row):
        here = pl.ds(row, ROWS)
        shares = {
            (d, dx): [frac_ref[d, part, pl.ds(row + dx, ROWS), :] for part in range(2)]
            for d in range(2)
            for dx in (-1, 0, 1)
        }
        planes = {
            dx: [(shares[0, dx][k] + shares[1, dx][k]) * (1.0 / 3.0) for k in range(2)] for dx in (-1, 0, 1)
        }
        for d in range(2):
            above, below = shares[d, 1], shares[d, -1]
            slope = [(above[k] - below[k]) * (1.0 / 6.0) for k in range(2)]
            ahead, behind = lateral(slope, -1, lane), lateral(slope, 1, lane)
            level = [planes[0][k] + (above[k] + below[k]) * (1.0 / 6.0) for k in range(2)]
            after, before = lateral(level, -1, lane), lateral(level, 1, lane)
            for part in range(2):
                gx = planes[1][part] - planes[-1][part] + ahead[part] + behind[part]
                gy = after[part] - before[part]
                recolor(d, part, here, shares[d, 0][part], gx, gy)

    def recolor(d, part, here, share, gx, gy):
        both, gap = gx + gy, gx - gy
        magnitude = jnp.sqrt(gx * gx + gy * gy)
        inverse = 1.0 / jnp.maximum(magnitude, gradient_floor)
        pull = half_tension * magnitude
        scale = half_tension * inverse
        added = {
            (0, 0): -pull,
            (1, 0): gx * gx * scale - pull,
            (0, 1): gy * gy * scale - pull,
            (1, 1): both * both * scale - pull,
            (1, -1): gap * gap * scale - pull,
        }
        mixing = mix_ref[d, part, here, :] * inverse
        diagonal = mixing * float(1.0 / np.sqrt(2.0))
        turned = {
            (1, 0, 0): mixing * gx,
            (0, 1, 0): mixing * gy,
            (1, 1, 0): diagonal * both,
            (1, -1, 0): diagonal * gap,
            (1, 0, 1): diagonal * gx,
            (0, 1, 1): diagonal * gy,
        }
        for q in range(19):
            a, b, c = (int(v) for v in velocity_table[q])
            remains = left_ref[q, d, part, here, :]
            sign = 1 if (a, b) > (0, 0) else -1
            key = (a * sign, b * sign) if (a, b) != (0, 0) else (0, 0)
            value = remains + pull if q == 0 else remains + added[key]
            total_ref[q, d, part, here, :] = value
            red = share * value
            if key != (0, 0):
                turn = turned[key[0], key[1], abs(c)]
                red = red + turn if sign > 0 else red - turn
            red_ref[q, d, part, here, :] = red

    def stream(row, d, parts):
        here = pl.ds(row, ROWS)
        totals, reds = [[], []], [[], []]
        for q in range(19):
            a, b, c = (int(v) for v in velocity_table[q])
            rows = pl.ds(row - a, ROWS)
            source = d if c == 0 else 1 - d
            if q:
                wall = [rock_ref[b + 1, source, part, rows, :] > 0.5 for part in range(parts)]
            for ref, found in ((total_ref, totals), (red_ref, reds)):
                if b == 0:
                    moved = [ref[q, source, part, rows, :] for part in range(parts)]
                else:
                    pair = [ref[q, source, part, rows, :] for part in range(2)]
                    edge = lane == (LANES - 1 if b > 0 else 0)
                    moved = [
                        pltpu.roll(jnp.where(edge, pair[1 - part], pair[part]), b % LANES, 1)
                        for part in range(parts)
                    ]
                for part in range(parts):
                    value = moved[part]
                    if q:
                        value = jnp.where(wall[part], ref[OPPOSITE[q], d, part, here, :], value)
                    found[part].append(value)
        return totals, reds

    def share_of(d, part, here, density_inverse, reds):
        rock = rock_ref[1, d, part, here, :] > 0.5
        return jnp.where(rock, label_ref[d, part, here, :], weighted_sum(reds) * density_inverse)

    def advance(row):
        here = pl.ds(row, ROWS)
        for d in range(2):
            totals, reds = stream(row, d, 2)
            for part in range(2):
                density, inverse, remains = relax(totals[part], rate)
                keep(d, part, here, density, share_of(d, part, here, inverse, reds[part]), remains)

    waiting = []
    for number in range(ROUNDS):
        fields = FIELDS if number == 0 else FIELDS - 1
        pack(number, fields)
        if number == 0:
            pl.semaphore_wait(barrier, len(offsets))
        waiting += exchange(number, fields)
        over_windows(0, EXTENT, functools.partial(start, number))
        for step in range(STEPS):
            low, high = 2 * step + 1, EXTENT - 2 * step - 1
            over_windows(low, high, collide)
            if step < STEPS - 1:
                over_windows(low + 1, high - 1, advance)
        for d in range(2):
            totals, reds = stream(HALO, d, 1)
            totals, reds = totals[0], reds[0]
            if number < ROUNDS - 1:
                inverse = 1.0 / weighted_sum(totals)
                for q in range(19):
                    states[number + 1][q, d, OWN, :] = totals[q]
                states[number + 1][19, d, OWN, :] = share_of(d, 0, OWN, inverse, reds)
            else:
                rock = rock_ref[1, d, 0, OWN, :] > 0.5
                label = label_ref[d, 0, OWN, :]
                for q in range(19):
                    first = states[0][q, d, OWN, :]
                    out[0, q, d] = jnp.where(rock, first, totals[q])
                    out[1, q, d] = jnp.where(rock, label * first, reds[q])
    for copy in waiting:
        copy.wait_send()


def body(populations, labels, solid, rates):
    anywhere = pl.BlockSpec(memory_space=pl.ANY)
    field = (2, 2, EXTENT, LANES)
    return pl.pallas_call(
        kernel,
        out_shape=jax.ShapeDtypeStruct((2, 19, 2, ROWS, LANES), jnp.float32),
        in_specs=[pl.BlockSpec(memory_space=pltpu.SMEM)] + [anywhere] * 3,
        out_specs=pl.BlockSpec(memory_space=pltpu.VMEM),
        scratch_shapes=[pltpu.VMEM((FIELDS, 2, EXTENT, LANES), jnp.float32)] * ROUNDS
        + [pltpu.VMEM((2, PACKED, EXTENT, LANES), jnp.float32)] * ROUNDS
        + [
            pltpu.VMEM((ROUNDS, 2, PACKED, ROWS, LANES), jnp.float32),
            pltpu.VMEM((2, 2, ROWS, LANES), jnp.int32),
            pltpu.VMEM((19,) + field, jnp.float32),
            pltpu.VMEM(field, jnp.float32),
            pltpu.VMEM(field, jnp.float32),
            pltpu.VMEM((19,) + field, jnp.float32),
            pltpu.VMEM((19,) + field, jnp.float32),
            pltpu.VMEM(field, jnp.float32),
            pltpu.VMEM((3,) + field, jnp.float32),
            pltpu.SemaphoreType.DMA((ROUNDS, 8)),
            pltpu.SemaphoreType.DMA((ROUNDS, 8)),
            pltpu.SemaphoreType.DMA((3,)),
        ],
        compiler_params=pltpu.CompilerParams(
            collective_id=0, has_side_effects=True, vmem_limit_bytes=32 * 2**20
        ),
    )(rates, populations, labels, solid)


def solution(mesh):
    return jax.shard_map(
        body,
        mesh=mesh,
        in_specs=(P(None, None, "gx", "gy"), P(None, "gx", "gy"), P(None, "gx", "gy"), P()),
        out_specs=P(None, None, None, "gx", "gy"),
        check_vma=False,
    )
```

```python
import functools

import jax
import jax.numpy as jnp
import numpy as np
from jax import lax
from jax.experimental import pallas as pl
from jax.experimental.pallas import tpu as pltpu
from jax.sharding import PartitionSpec as P

ITERS = 6
ROUNDS = 2
STEPS = ITERS // ROUNDS
HALO = 2 * STEPS
MESH = pl.DeviceIdType.MESH

velocity_table = np.array(
    [
        [0, 0, 0],
        [1, 0, 0],
        [-1, 0, 0],
        [0, 1, 0],
        [0, -1, 0],
        [0, 0, 1],
        [0, 0, -1],
        [1, 1, 0],
        [-1, -1, 0],
        [1, -1, 0],
        [-1, 1, 0],
        [1, 0, 1],
        [-1, 0, -1],
        [1, 0, -1],
        [-1, 0, 1],
        [0, 1, 1],
        [0, -1, -1],
        [0, 1, -1],
        [0, -1, 1],
    ]
)
half_tension = 0.05
recolor_beta = 0.7
gradient_floor = 0.1
ROWS = 8
LANES = 128
EXTENT = ROWS + 2 * HALO
CHUNK = 16
PER_STRIP = LANES // CHUNK
FIELDS = 21
PACKED = -(-2 * FIELDS // PER_STRIP)
PACKED_LATER = -(-2 * (FIELDS - 1) // PER_STRIP)
OWN = slice(HALO, HALO + ROWS)


def opposite_of(member):
    return int(np.argmax(np.all(velocity_table == -velocity_table[member], axis=1)))


OPPOSITE = [opposite_of(member) for member in range(19)]


def placement(dx):
    first = HALO - ROWS * dx
    low, high = max(first, 0), min(first + ROWS, EXTENT)
    return low - first, low, high - low


def lateral(pair, dy, lane):
    if dy == 0:
        return pair
    edge = lane == (LANES - 1 if dy > 0 else 0)
    return [
        pltpu.roll(jnp.where(edge, pair[1 - part], pair[part]), dy % LANES, 1) for part in range(2)
    ]


def relax(f, rate):
    plus = {q: f[q] + f[q + 1] for q in range(1, 19, 2)}
    minus = {q: f[q] - f[q + 1] for q in range(1, 19, 2)}
    both = {q: plus[q] + plus[q + 2] for q in (7, 11, 15)}
    cross = {q: plus[q] - plus[q + 2] for q in (7, 11, 15)}
    head = {q: minus[q] + minus[q + 2] for q in (7, 11, 15)}
    tail = {q: minus[q] - minus[q + 2] for q in (7, 11, 15)}
    axes = plus[1] + plus[3] + plus[5]
    diagonals = both[7] + both[11] + both[15]
    density = f[0] * (1.0 / 3.0) + axes * (1.0 / 18.0) + diagonals * (1.0 / 36.0)
    momentum = [
        minus[1] * (1.0 / 18.0) + (head[7] + head[11]) * (1.0 / 36.0),
        minus[3] * (1.0 / 18.0) + (tail[7] + head[15]) * (1.0 / 36.0),
        minus[5] * (1.0 / 18.0) + (tail[11] + tail[15]) * (1.0 / 36.0),
    ]
    inverse = 1.0 / density
    speed = [part * inverse for part in momentum]
    xx, yy, zz = (momentum[k] * speed[k] for k in range(3))
    xy, yz, xz = momentum[0] * speed[1], momentum[1] * speed[2], momentum[0] * speed[2]
    square = xx + yy + zz
    energy = f[0] * -10.0 + axes * (-11.0 / 18.0) + diagonals * (8.0 / 36.0) - (19.0 * square - 11.0 * density)
    fourth = f[0] * 4.0 + axes * (-4.0 / 18.0) + diagonals * (1.0 / 36.0) - (3.0 * density - 5.5 * square)
    first_axis = (3.0 * plus[1] - axes) * (1.0 / 18.0)
    first_diag = (diagonals - 3.0 * both[15]) * (1.0 / 36.0)
    first_flow = 3.0 * xx - square
    second_axis = (plus[3] - plus[5]) * (1.0 / 18.0)
    second_diag = (both[7] - both[11]) * (1.0 / 36.0)
    second_flow = yy - zz
    energy = energy * (rate[0] * (1.0 / 2394.0))
    fourth = fourth * (rate[1] * (1.0 / 252.0))
    first = (first_axis + first_diag - first_flow) * (rate[5] * (1.0 / 36.0))
    first_high = (first_diag - 2.0 * first_axis + 0.5 * first_flow) * (rate[6] * (1.0 / 72.0))
    second = (second_axis + second_diag - second_flow) * (rate[7] * (1.0 / 12.0))
    second_high = (second_diag - 2.0 * second_axis + 0.5 * second_flow) * (rate[8] * (1.0 / 24.0))
    on_rest = energy * -90.0 + fourth * 36.0
    on_axes = energy * -198.0 - fourth * 72.0
    on_diagonals = energy * 288.0 + fourth * 36.0
    axis_first = (first - 2.0 * first_high) * 18.0
    axis_second = (second - 2.0 * second_high) * 18.0
    diag_first = (first + first_high) * 36.0
    diag_second = (second + second_high) * 36.0
    rest_axes = on_axes - axis_first
    along = [on_axes + 2.0 * axis_first, rest_axes + axis_second, rest_axes - axis_second]
    near = on_diagonals + diag_first
    around = {7: near + diag_second, 11: near - diag_second, 15: on_diagonals - 2.0 * diag_first}
    shear = {
        7: (cross[7] * (1.0 / 36.0) - xy) * (rate[9] * 9.0),
        15: (cross[15] * (1.0 / 36.0) - yz) * (rate[10] * 9.0),
        11: (cross[11] * (1.0 / 36.0) - xz) * (rate[11] * 9.0),
    }
    flux = []
    for k, diag in enumerate((head[7] + head[11], tail[7] + head[15], tail[11] + tail[15])):
        moment = minus[2 * k + 1] * (-4.0 / 18.0) + diag * (1.0 / 36.0) + momentum[k] * (2.0 / 3.0)
        flux.append(moment * (rate[2 + k] * 0.9))
    twist = [
        (head[7] - head[11]) * (rate[12] * (4.5 / 36.0)),
        (head[15] - tail[7]) * (rate[13] * (4.5 / 36.0)),
        (tail[11] - tail[15]) * (rate[14] * (4.5 / 36.0)),
    ]
    left = [None] * 19
    left[0] = f[0] - on_rest
    for k in range(3):
        double = 2.0 * flux[k]
        left[2 * k + 1] = f[2 * k + 1] - (along[k] - double)
        left[2 * k + 2] = f[2 * k + 2] - (along[k] + double)
    odd = {
        7: (flux[0] + twist[0], flux[1] - twist[1]),
        11: (flux[0] - twist[0], flux[2] + twist[2]),
        15: (flux[1] + twist[1], flux[2] - twist[2]),
    }
    for q in (7, 11, 15):
        same, other = around[q] + shear[q], around[q] - shear[q]
        total, gap = odd[q][0] + odd[q][1], odd[q][0] - odd[q][1]
        left[q] = f[q] - (same + total)
        left[q + 1] = f[q + 1] - (same - total)
        left[q + 2] = f[q + 2] - (other + gap)
        left[q + 3] = f[q + 3] - (other - gap)
    return density, inverse, left


def weighted_sum(f):
    axes = functools.reduce(lambda a, b: a + b, f[1:7])
    diagonals = functools.reduce(lambda a, b: a + b, f[7:19])
    return f[0] * (1.0 / 3.0) + axes * (1.0 / 18.0) + diagonals * (1.0 / 36.0)


def over_windows(low, high, work):
    for index in range(-(-(high - low) // ROWS)):
        work(min(low + ROWS * index, high - ROWS))


def kernel(
    rate_hbm, pop_hbm, label_hbm, solid_hbm, out, *scratch
):
    states = scratch[:ROUNDS]
    strips, edges, packs, codes, rate_ref, left_ref, frac_ref, mix_ref, total_ref, red_ref, label_ref, rock_ref, send, recv, local = scratch[ROUNDS:]
    gx, gy = lax.axis_index("gx"), lax.axis_index("gy")
    nx, ny = lax.axis_size("gx"), lax.axis_size("gy")
    offsets = [(1, 0), (-1, 0), (0, 1), (0, -1)]
    device = {
        (dx, dy): (lax.rem(gx + (dx + nx), nx), lax.rem(gy + (dy + ny), ny)) for dx, dy in offsets
    }
    barrier = pltpu.get_barrier_semaphore()
    for offset in offsets:
        pl.semaphore_signal(barrier, inc=1, device_id=device[offset], device_id_type=MESH)
    loads = [
        pltpu.make_async_copy(rate_hbm, rate_ref, local.at[3]),
        pltpu.make_async_copy(label_hbm, codes.at[0], local.at[1]),
        pltpu.make_async_copy(solid_hbm, codes.at[1], local.at[2]),
        pltpu.make_async_copy(pop_hbm, states[0].at[0:19, :, OWN, :], local.at[0]),
    ]
    for copy in loads:
        copy.start()
    for copy in loads:
        copy.wait()
    for d in range(2):
        states[0][19, d, OWN, :] = codes[0, d].astype(jnp.float32)
        states[0][20, d, OWN, :] = jnp.where(codes[1, d] > 0, 1.0, 0.0)

    rate = [rate_ref[k] for k in range(15)]
    lane = lax.broadcasted_iota(jnp.int32, (ROWS, LANES), 1)
    chunk = lane // CHUNK
    turned_chunk = lax.rem(lane + CHUNK // 2, LANES) // CHUNK
    right_half = lane < LANES // 2

    def pack():
        for first in range(0, 2 * FIELDS, PER_STRIP):
            to_left = to_right = None
            for slot in range(min(PER_STRIP, 2 * FIELDS - first)):
                plane = first + slot
                value = states[0][plane // 2, plane % 2, OWN, :]
                moved = value if slot == 0 else pltpu.roll(value, CHUNK * slot, 1)
                to_left = moved if slot == 0 else jnp.where(chunk == slot, moved, to_left)
                before = (slot - 1) % PER_STRIP
                to_right = moved if slot == 0 else jnp.where(chunk == before, moved, to_right)
            packs[0, first // PER_STRIP] = to_right
            packs[1, first // PER_STRIP] = to_left

    def pack_edges(planes):
        for first in range(0, len(planes), PER_STRIP):
            packed = planes[first]
            for slot in range(1, min(PER_STRIP, len(planes) - first)):
                moved = pltpu.roll(planes[first + slot], CHUNK * slot, 1)
                packed = jnp.where(turned_chunk == slot, moved, packed)
            edges[0, first // PER_STRIP, OWN, :] = packed

    copies = []

    def push(source, target, offset):
        place = len(copies)
        copy = pltpu.make_async_remote_copy(
            src_ref=source,
            dst_ref=target,
            send_sem=send.at[place],
            recv_sem=recv.at[place],
            device_id=device[offset],
            device_id_type=MESH,
        )
        copy.start()
        copies.append(copy)
        return copy

    def push_rows(number, fields, dx):
        begin, low, count = placement(dx)
        share = push(
            states[number].at[19:fields, :, HALO + begin : HALO + begin + count, :],
            states[number].at[19:fields, :, low : low + count, :],
            (dx, 0),
        )
        if dx > 0:
            begin, low = begin + 1, low + 1
        count = count - 1
        return [share, push(
            states[number].at[0:19, :, HALO + begin : HALO + begin + count, :],
            states[number].at[0:19, :, low : low + count, :],
            (dx, 0),
        )]

    def push_strip(dy):
        side = 0 if dy > 0 else 1
        return push(packs.at[side], strips.at[side, :, OWN, :], (0, dy))

    def pass_on(strips_ref, dx):
        begin, low, count = placement(dx)
        return push(
            strips_ref.at[:, :, HALO + begin : HALO + begin + count, :],
            strips_ref.at[:, :, low : low + count, :],
            (dx, 0),
        )

    def exchange(number):
        if number == 0:
            beside = [push_strip(dy) for dy in (1, -1)]
        else:
            rows = [pass_on(edges, dx) for dx in (1, -1)]
        fields = FIELDS if number == 0 else FIELDS - 1
        sent = push_rows(number, fields, 1) + push_rows(number, fields, -1)
        if number == 0:
            for copy in beside:
                copy.wait_recv()
            rows = [pass_on(strips, dx) for dx in (1, -1)]
        for copy in sent + rows:
            copy.wait_recv()

    def strip(number, field, d, rows):
        plane = 2 * field + d
        which, slot = plane // PER_STRIP, plane % PER_STRIP
        if number == 0:
            moved = [strips[side, which, rows, :] for side in range(2)]
        else:
            moved = [edges[0, which, rows, :]]
        if slot:
            moved = [pltpu.roll(value, LANES - CHUNK * slot, 1) for value in moved]
        return moved[0] if number else jnp.where(right_half, moved[1], moved[0])

    def keep(d, part, rows, density, share, remains):
        frac_ref[d, part, rows, :] = share
        mix_ref[d, part, rows, :] = recolor_beta * density * share * (1.0 - share)
        for q in range(19):
            left_ref[q, d, part, rows, :] = remains[q]

    def start(number, row):
        rows = pl.ds(row, ROWS)
        for d in range(2):

            def both_of(field):
                return [states[number][field, d, rows, :], strip(number, field, d, rows)]

            share = both_of(19)
            if number == 0:
                rock = both_of(20)
                for dy in (-1, 0, 1):
                    moved = lateral(rock, dy, lane)
                    for part in range(2):
                        rock_ref[dy + 1, d, part, rows, :] = moved[part]
                for part in range(2):
                    label_ref[d, part, rows, :] = share[part]
            f = [both_of(q) for q in range(19)]
            for part in range(2):
                density, _, remains = relax([pair[part] for pair in f], rate)
                keep(d, part, rows, density, share[part], remains)

    def collide(row):
        here = pl.ds(row, ROWS)
        shares = {
            (d, dx): [frac_ref[d, part, pl.ds(row + dx, ROWS), :] for part in range(2)]
            for d in range(2)
            for dx in (-1, 0, 1)
        }
        planes = {
            dx: [(shares[0, dx][k] + shares[1, dx][k]) * (1.0 / 3.0) for k in range(2)] for dx in (-1, 0, 1)
        }
        for d in range(2):
            above, below = shares[d, 1], shares[d, -1]
            slope = [(above[k] - below[k]) * (1.0 / 6.0) for k in range(2)]
            ahead, behind = lateral(slope, -1, lane), lateral(slope, 1, lane)
            level = [planes[0][k] + (above[k] + below[k]) * (1.0 / 6.0) for k in range(2)]
            after, before = lateral(level, -1, lane), lateral(level, 1, lane)
            for part in range(2):
                gx = planes[1][part] - planes[-1][part] + ahead[part] + behind[part]
                gy = after[part] - before[part]
                recolor(d, part, here, shares[d, 0][part], gx, gy)

    def recolor(d, part, here, share, gx, gy):
        both, gap = gx + gy, gx - gy
        magnitude = jnp.sqrt(gx * gx + gy * gy)
        inverse = 1.0 / jnp.maximum(magnitude, gradient_floor)
        pull = half_tension * magnitude
        scale = half_tension * inverse
        added = {
            (0, 0): -pull,
            (1, 0): gx * gx * scale - pull,
            (0, 1): gy * gy * scale - pull,
            (1, 1): both * both * scale - pull,
            (1, -1): gap * gap * scale - pull,
        }
        mixing = mix_ref[d, part, here, :] * inverse
        diagonal = mixing * float(1.0 / np.sqrt(2.0))
        turned = {
            (1, 0, 0): mixing * gx,
            (0, 1, 0): mixing * gy,
            (1, 1, 0): diagonal * both,
            (1, -1, 0): diagonal * gap,
            (1, 0, 1): diagonal * gx,
            (0, 1, 1): diagonal * gy,
        }
        for q in range(19):
            a, b, c = (int(v) for v in velocity_table[q])
            remains = left_ref[q, d, part, here, :]
            sign = 1 if (a, b) > (0, 0) else -1
            key = (a * sign, b * sign) if (a, b) != (0, 0) else (0, 0)
            value = remains + pull if q == 0 else remains + added[key]
            total_ref[q, d, part, here, :] = value
            red = share * value
            if key != (0, 0):
                turn = turned[key[0], key[1], abs(c)]
                red = red + turn if sign > 0 else red - turn
            red_ref[q, d, part, here, :] = red

    def stream(row, d, parts):
        here = pl.ds(row, ROWS)
        totals, reds = [[], []], [[], []]
        for q in range(19):
            a, b, c = (int(v) for v in velocity_table[q])
            rows = pl.ds(row - a, ROWS)
            source = d if c == 0 else 1 - d
            if q:
                wall = [rock_ref[b + 1, source, part, rows, :] > 0.5 for part in range(parts)]
            for ref, found in ((total_ref, totals), (red_ref, reds)):
                if b == 0:
                    moved = [ref[q, source, part, rows, :] for part in range(parts)]
                else:
                    pair = [ref[q, source, part, rows, :] for part in range(2)]
                    edge = lane == (LANES - 1 if b > 0 else 0)
                    moved = [
                        pltpu.roll(jnp.where(edge, pair[1 - part], pair[part]), b % LANES, 1)
                        for part in range(parts)
                    ]
                for part in range(parts):
                    value = moved[part]
                    if q:
                        value = jnp.where(wall[part], ref[OPPOSITE[q], d, part, here, :], value)
                    found[part].append(value)
        return totals, reds

    def share_of(d, part, here, density_inverse, reds):
        rock = rock_ref[1, d, part, here, :] > 0.5
        return jnp.where(rock, label_ref[d, part, here, :], weighted_sum(reds) * density_inverse)

    def advance(row):
        here = pl.ds(row, ROWS)
        for d in range(2):
            totals, reds = stream(row, d, 2)
            for part in range(2):
                density, inverse, remains = relax(totals[part], rate)
                keep(d, part, here, density, share_of(d, part, here, inverse, reds[part]), remains)

    for number in range(ROUNDS):
        if number == 0:
            pack()
            pl.semaphore_wait(barrier, len(offsets))
        exchange(number)
        over_windows(0, EXTENT, functools.partial(start, number))
        for step in range(STEPS):
            low, high = 2 * step + 1, EXTENT - 2 * step - 1
            over_windows(low, high, collide)
            if step < STEPS - 1:
                over_windows(low + 1, high - 1, advance)
        if number < ROUNDS - 1:
            borders = [None] * (2 * (FIELDS - 1))
            for d in range(2):
                totals, reds = stream(HALO, d, 2)
                share = [
                    share_of(d, part, OWN, 1.0 / weighted_sum(totals[part]), reds[part]) for part in range(2)
                ]
                for q in range(19):
                    states[number + 1][q, d, OWN, :] = totals[0][q]
                    borders[2 * q + d] = totals[1][q]
                states[number + 1][19, d, OWN, :] = share[0]
                borders[2 * 19 + d] = share[1]
            pack_edges(borders)
        else:
            for d in range(2):
                totals, reds = stream(HALO, d, 1)
                rock = rock_ref[1, d, 0, OWN, :] > 0.5
                label = label_ref[d, 0, OWN, :]
                for q in range(19):
                    first = states[0][q, d, OWN, :]
                    out[0, q, d] = jnp.where(rock, first, totals[0][q])
                    out[1, q, d] = jnp.where(rock, label * first, reds[0][q])
    for copy in copies:
        copy.wait_send()


def body(populations, labels, solid, rates):
    in_place = pl.BlockSpec(memory_space=pl.ANY)
    field = (2, 2, EXTENT, LANES)
    return pl.pallas_call(
        kernel,
        out_shape=jax.ShapeDtypeStruct((2, 19, 2, ROWS, LANES), jnp.float32),
        in_specs=[in_place] * 4,
        out_specs=pl.BlockSpec(memory_space=pltpu.VMEM),
        scratch_shapes=[pltpu.VMEM((FIELDS, 2, EXTENT, LANES), jnp.float32)] * ROUNDS
        + [
            pltpu.VMEM((2, PACKED, EXTENT, LANES), jnp.float32),
            pltpu.VMEM((1, PACKED_LATER, EXTENT, LANES), jnp.float32),
            pltpu.VMEM((2, PACKED, ROWS, LANES), jnp.float32),
            pltpu.VMEM((2, 2, ROWS, LANES), jnp.int32),
            pltpu.SMEM((15,), jnp.float32),
            pltpu.VMEM((19,) + field, jnp.float32),
            pltpu.VMEM(field, jnp.float32),
            pltpu.VMEM(field, jnp.float32),
            pltpu.VMEM((19,) + field, jnp.float32),
            pltpu.VMEM((19,) + field, jnp.float32),
            pltpu.VMEM(field, jnp.float32),
            pltpu.VMEM((3,) + field, jnp.float32),
            pltpu.SemaphoreType.DMA((20,)),
            pltpu.SemaphoreType.DMA((20,)),
            pltpu.SemaphoreType.DMA((4,)),
        ],
        compiler_params=pltpu.CompilerParams(
            collective_id=0, has_side_effects=True, vmem_limit_bytes=32 * 2**20
        ),
    )(*[pltpu.with_memory_space_constraint(x, pltpu.HBM) for x in (rates, populations, labels, solid)])


def solution(mesh):
    return jax.shard_map(
        body,
        mesh=mesh,
        in_specs=(P(None, None, "gx", "gy"), P(None, "gx", "gy"), P(None, "gx", "gy"), P()),
        out_specs=P(None, None, None, "gx", "gy"),
        check_vma=False,
    )
```

```python
import functools

import jax
import jax.numpy as jnp
import numpy as np
from jax import lax
from jax.experimental import pallas as pl
from jax.experimental.pallas import tpu as pltpu
from jax.sharding import PartitionSpec as P

ITERS = 6
ROUNDS = 2
STEPS = ITERS // ROUNDS
HALO = 2 * STEPS
MESH = pl.DeviceIdType.MESH

velocity_table = np.array(
    [
        [0, 0, 0],
        [1, 0, 0],
        [-1, 0, 0],
        [0, 1, 0],
        [0, -1, 0],
        [0, 0, 1],
        [0, 0, -1],
        [1, 1, 0],
        [-1, -1, 0],
        [1, -1, 0],
        [-1, 1, 0],
        [1, 0, 1],
        [-1, 0, -1],
        [1, 0, -1],
        [-1, 0, 1],
        [0, 1, 1],
        [0, -1, -1],
        [0, 1, -1],
        [0, -1, 1],
    ]
)
half_tension = 0.05
recolor_beta = 0.7
gradient_floor = 0.1
ROWS = 8
LANES = 128
EXTENT = ROWS + 2 * HALO
CHUNK = 12
PER_STRIP = LANES // CHUNK
FIELDS = 21
PACKED = -(-2 * FIELDS // PER_STRIP)
PACKED_LATER = -(-2 * (FIELDS - 1) // PER_STRIP)
OWN = slice(HALO, HALO + ROWS)


def opposite_of(member):
    return int(np.argmax(np.all(velocity_table == -velocity_table[member], axis=1)))


OPPOSITE = [opposite_of(member) for member in range(19)]


def placement(dx):
    first = HALO - ROWS * dx
    low, high = max(first, 0), min(first + ROWS, EXTENT)
    return low - first, low, high - low


def lateral(pair, dy, lane):
    if dy == 0:
        return pair
    edge = lane == (LANES - 1 if dy > 0 else 0)
    return [
        pltpu.roll(jnp.where(edge, pair[1 - part], pair[part]), dy % LANES, 1) for part in range(2)
    ]


def relax(f, rate):
    plus = {q: f[q] + f[q + 1] for q in range(1, 19, 2)}
    minus = {q: f[q] - f[q + 1] for q in range(1, 19, 2)}
    both = {q: plus[q] + plus[q + 2] for q in (7, 11, 15)}
    cross = {q: plus[q] - plus[q + 2] for q in (7, 11, 15)}
    head = {q: minus[q] + minus[q + 2] for q in (7, 11, 15)}
    tail = {q: minus[q] - minus[q + 2] for q in (7, 11, 15)}
    axes = plus[1] + plus[3] + plus[5]
    diagonals = both[7] + both[11] + both[15]
    density = f[0] * (1.0 / 3.0) + axes * (1.0 / 18.0) + diagonals * (1.0 / 36.0)
    momentum = [
        minus[1] * (1.0 / 18.0) + (head[7] + head[11]) * (1.0 / 36.0),
        minus[3] * (1.0 / 18.0) + (tail[7] + head[15]) * (1.0 / 36.0),
        minus[5] * (1.0 / 18.0) + (tail[11] + tail[15]) * (1.0 / 36.0),
    ]
    inverse = 1.0 / density
    speed = [part * inverse for part in momentum]
    xx, yy, zz = (momentum[k] * speed[k] for k in range(3))
    xy, yz, xz = momentum[0] * speed[1], momentum[1] * speed[2], momentum[0] * speed[2]
    square = xx + yy + zz
    energy = f[0] * -10.0 + axes * (-11.0 / 18.0) + diagonals * (8.0 / 36.0) - (19.0 * square - 11.0 * density)
    fourth = f[0] * 4.0 + axes * (-4.0 / 18.0) + diagonals * (1.0 / 36.0) - (3.0 * density - 5.5 * square)
    first_axis = (3.0 * plus[1] - axes) * (1.0 / 18.0)
    first_diag = (diagonals - 3.0 * both[15]) * (1.0 / 36.0)
    first_flow = 3.0 * xx - square
    second_axis = (plus[3] - plus[5]) * (1.0 / 18.0)
    second_diag = (both[7] - both[11]) * (1.0 / 36.0)
    second_flow = yy - zz
    energy = energy * (rate[0] * (1.0 / 2394.0))
    fourth = fourth * (rate[1] * (1.0 / 252.0))
    first = (first_axis + first_diag - first_flow) * (rate[5] * (1.0 / 36.0))
    first_high = (first_diag - 2.0 * first_axis + 0.5 * first_flow) * (rate[6] * (1.0 / 72.0))
    second = (second_axis + second_diag - second_flow) * (rate[7] * (1.0 / 12.0))
    second_high = (second_diag - 2.0 * second_axis + 0.5 * second_flow) * (rate[8] * (1.0 / 24.0))
    on_rest = energy * -90.0 + fourth * 36.0
    on_axes = energy * -198.0 - fourth * 72.0
    on_diagonals = energy * 288.0 + fourth * 36.0
    axis_first = (first - 2.0 * first_high) * 18.0
    axis_second = (second - 2.0 * second_high) * 18.0
    diag_first = (first + first_high) * 36.0
    diag_second = (second + second_high) * 36.0
    rest_axes = on_axes - axis_first
    along = [on_axes + 2.0 * axis_first, rest_axes + axis_second, rest_axes - axis_second]
    near = on_diagonals + diag_first
    around = {7: near + diag_second, 11: near - diag_second, 15: on_diagonals - 2.0 * diag_first}
    shear = {
        7: (cross[7] * (1.0 / 36.0) - xy) * (rate[9] * 9.0),
        15: (cross[15] * (1.0 / 36.0) - yz) * (rate[10] * 9.0),
        11: (cross[11] * (1.0 / 36.0) - xz) * (rate[11] * 9.0),
    }
    flux = []
    for k, diag in enumerate((head[7] + head[11], tail[7] + head[15], tail[11] + tail[15])):
        moment = minus[2 * k + 1] * (-4.0 / 18.0) + diag * (1.0 / 36.0) + momentum[k] * (2.0 / 3.0)
        flux.append(moment * (rate[2 + k] * 0.9))
    twist = [
        (head[7] - head[11]) * (rate[12] * (4.5 / 36.0)),
        (head[15] - tail[7]) * (rate[13] * (4.5 / 36.0)),
        (tail[11] - tail[15]) * (rate[14] * (4.5 / 36.0)),
    ]
    left = [None] * 19
    left[0] = f[0] - on_rest
    for k in range(3):
        double = 2.0 * flux[k]
        left[2 * k + 1] = f[2 * k + 1] - (along[k] - double)
        left[2 * k + 2] = f[2 * k + 2] - (along[k] + double)
    odd = {
        7: (flux[0] + twist[0], flux[1] - twist[1]),
        11: (flux[0] - twist[0], flux[2] + twist[2]),
        15: (flux[1] + twist[1], flux[2] - twist[2]),
    }
    for q in (7, 11, 15):
        same, other = around[q] + shear[q], around[q] - shear[q]
        total, gap = odd[q][0] + odd[q][1], odd[q][0] - odd[q][1]
        left[q] = f[q] - (same + total)
        left[q + 1] = f[q + 1] - (same - total)
        left[q + 2] = f[q + 2] - (other + gap)
        left[q + 3] = f[q + 3] - (other - gap)
    return density, inverse, left


def weighted_sum(f):
    axes = functools.reduce(lambda a, b: a + b, f[1:7])
    diagonals = functools.reduce(lambda a, b: a + b, f[7:19])
    return f[0] * (1.0 / 3.0) + axes * (1.0 / 18.0) + diagonals * (1.0 / 36.0)


def over_windows(low, high, work):
    for index in range(-(-(high - low) // ROWS)):
        work(min(low + ROWS * index, high - ROWS))


def kernel(
    rate_hbm, pop_hbm, label_hbm, solid_hbm, out, *scratch
):
    states = scratch[:ROUNDS]
    strips, edges, packs, codes, rate_ref, left_ref, frac_ref, mix_ref, total_ref, red_ref, label_ref, rock_ref, send, recv, local = scratch[ROUNDS:]
    gx, gy = lax.axis_index("gx"), lax.axis_index("gy")
    nx, ny = lax.axis_size("gx"), lax.axis_size("gy")
    offsets = [(1, 0), (-1, 0), (0, 1), (0, -1)]
    device = {
        (dx, dy): (lax.rem(gx + (dx + nx), nx), lax.rem(gy + (dy + ny), ny)) for dx, dy in offsets
    }
    barrier = pltpu.get_barrier_semaphore()
    for offset in offsets:
        pl.semaphore_signal(barrier, inc=1, device_id=device[offset], device_id_type=MESH)
    loads = [
        pltpu.make_async_copy(rate_hbm, rate_ref, local.at[3]),
        pltpu.make_async_copy(label_hbm, codes.at[0], local.at[1]),
        pltpu.make_async_copy(solid_hbm, codes.at[1], local.at[2]),
        pltpu.make_async_copy(pop_hbm, states[0].at[0:19, :, OWN, :], local.at[0]),
    ]
    for copy in loads:
        copy.start()
    for copy in loads:
        copy.wait()
    for d in range(2):
        states[0][19, d, OWN, :] = codes[0, d].astype(jnp.float32)
        states[0][20, d, OWN, :] = jnp.where(codes[1, d] > 0, 1.0, 0.0)

    rate = [rate_ref[k] for k in range(15)]
    lane = lax.broadcasted_iota(jnp.int32, (ROWS, LANES), 1)
    chunk = lane // CHUNK
    turned_chunk = lax.rem(lane + CHUNK // 2, LANES) // CHUNK
    right_half = lane < LANES // 2

    def pack():
        for first in range(0, 2 * FIELDS, PER_STRIP):
            to_left = to_right = None
            for slot in range(min(PER_STRIP, 2 * FIELDS - first)):
                plane = first + slot
                value = states[0][plane // 2, plane % 2, OWN, :]
                moved = value if slot == 0 else pltpu.roll(value, CHUNK * slot, 1)
                to_left = moved if slot == 0 else jnp.where(chunk == slot, moved, to_left)
                before = (slot - 1) % PER_STRIP
                to_right = moved if slot == 0 else jnp.where(chunk == before, moved, to_right)
            packs[0, first // PER_STRIP] = to_right
            packs[1, first // PER_STRIP] = to_left

    def pack_edges(planes):
        for first in range(0, len(planes), PER_STRIP):
            packed = planes[first]
            for slot in range(1, min(PER_STRIP, len(planes) - first)):
                moved = pltpu.roll(planes[first + slot], CHUNK * slot, 1)
                packed = jnp.where(turned_chunk == slot, moved, packed)
            edges[0, first // PER_STRIP, OWN, :] = packed

    copies = []

    def push(source, target, offset):
        place = len(copies)
        copy = pltpu.make_async_remote_copy(
            src_ref=source,
            dst_ref=target,
            send_sem=send.at[place],
            recv_sem=recv.at[place],
            device_id=device[offset],
            device_id_type=MESH,
        )
        copy.start()
        copies.append(copy)
        return copy

    def push_rows(number, fields, dx):
        begin, low, count = placement(dx)
        share = push(
            states[number].at[19:fields, :, HALO + begin : HALO + begin + count, :],
            states[number].at[19:fields, :, low : low + count, :],
            (dx, 0),
        )
        if dx > 0:
            begin, low = begin + 1, low + 1
        count = count - 1
        return [share, push(
            states[number].at[0:19, :, HALO + begin : HALO + begin + count, :],
            states[number].at[0:19, :, low : low + count, :],
            (dx, 0),
        )]

    def push_strip(dy):
        side = 0 if dy > 0 else 1
        return push(packs.at[side], strips.at[side, :, OWN, :], (0, dy))

    def pass_on(strips_ref, dx, side):
        begin, low, count = placement(dx)
        return push(
            strips_ref.at[side, :, HALO + begin : HALO + begin + count, :],
            strips_ref.at[side, :, low : low + count, :],
            (dx, 0),
        )

    def strip(number, field, d, rows):
        plane = 2 * field + d
        which, slot = plane // PER_STRIP, plane % PER_STRIP
        if number == 0:
            moved = [strips[side, which, rows, :] for side in range(2)]
        else:
            moved = [edges[0, which, rows, :]]
        if slot:
            moved = [pltpu.roll(value, LANES - CHUNK * slot, 1) for value in moved]
        return moved[0] if number else jnp.where(right_half, moved[1], moved[0])

    def keep(d, part, rows, density, share, remains):
        frac_ref[d, part, rows, :] = share
        mix_ref[d, part, rows, :] = recolor_beta * density * share * (1.0 - share)
        for q in range(19):
            left_ref[q, d, part, rows, :] = remains[q]

    def start(number, part, row):
        rows = pl.ds(row, ROWS)
        for d in range(2):

            def cells(field):
                return states[number][field, d, rows, :] if part == 0 else strip(number, field, d, rows)

            share = cells(19)
            if number == 0:
                label_ref[d, part, rows, :] = share
            density, _, remains = relax([cells(q) for q in range(19)], rate)
            keep(d, part, rows, density, share, remains)

    def walls(row):
        rows = pl.ds(row, ROWS)
        for d in range(2):
            rock = [states[0][20, d, rows, :], strip(0, 20, d, rows)]
            for dy in (-1, 0, 1):
                moved = lateral(rock, dy, lane)
                for part in range(2):
                    rock_ref[dy + 1, d, part, rows, :] = moved[part]

    def begin_round(number):
        outer = (0, EXTENT - ROWS)
        if number == 0:
            beside = [push_strip(dy) for dy in (1, -1)]
            sent = push_rows(0, FIELDS, 1) + push_rows(0, FIELDS, -1)
            start(0, 0, HALO)
            corners = []
            for side, copy in enumerate(beside):
                copy.wait_recv()
                corners += [pass_on(strips, dx, side) for dx in (1, -1)]
            start(0, 1, HALO)
        else:
            corners = [pass_on(edges, dx, 0) for dx in (1, -1)]
            sent = push_rows(number, FIELDS - 1, 1) + push_rows(number, FIELDS - 1, -1)
            start(number, 0, HALO)
            start(number, 1, HALO)
        for copy in sent:
            copy.wait_recv()
        for row in outer:
            start(number, 0, row)
        for copy in corners:
            copy.wait_recv()
        for row in outer:
            start(number, 1, row)
        if number == 0:
            over_windows(0, EXTENT, walls)

    def collide(row):
        here = pl.ds(row, ROWS)
        shares = {
            (d, dx): [frac_ref[d, part, pl.ds(row + dx, ROWS), :] for part in range(2)]
            for d in range(2)
            for dx in (-1, 0, 1)
        }
        planes = {
            dx: [(shares[0, dx][k] + shares[1, dx][k]) * (1.0 / 3.0) for k in range(2)] for dx in (-1, 0, 1)
        }
        for d in range(2):
            above, below = shares[d, 1], shares[d, -1]
            slope = [(above[k] - below[k]) * (1.0 / 6.0) for k in range(2)]
            ahead, behind = lateral(slope, -1, lane), lateral(slope, 1, lane)
            level = [planes[0][k] + (above[k] + below[k]) * (1.0 / 6.0) for k in range(2)]
            after, before = lateral(level, -1, lane), lateral(level, 1, lane)
            for part in range(2):
                gx = planes[1][part] - planes[-1][part] + ahead[part] + behind[part]
                gy = after[part] - before[part]
                recolor(d, part, here, shares[d, 0][part], gx, gy)

    def recolor(d, part, here, share, gx, gy):
        both, gap = gx + gy, gx - gy
        magnitude = jnp.sqrt(gx * gx + gy * gy)
        inverse = 1.0 / jnp.maximum(magnitude, gradient_floor)
        pull = half_tension * magnitude
        scale = half_tension * inverse
        added = {
            (0, 0): -pull,
            (1, 0): gx * gx * scale - pull,
            (0, 1): gy * gy * scale - pull,
            (1, 1): both * both * scale - pull,
            (1, -1): gap * gap * scale - pull,
        }
        mixing = mix_ref[d, part, here, :] * inverse
        diagonal = mixing * float(1.0 / np.sqrt(2.0))
        turned = {
            (1, 0, 0): mixing * gx,
            (0, 1, 0): mixing * gy,
            (1, 1, 0): diagonal * both,
            (1, -1, 0): diagonal * gap,
            (1, 0, 1): diagonal * gx,
            (0, 1, 1): diagonal * gy,
        }
        for q in range(19):
            a, b, c = (int(v) for v in velocity_table[q])
            remains = left_ref[q, d, part, here, :]
            sign = 1 if (a, b) > (0, 0) else -1
            key = (a * sign, b * sign) if (a, b) != (0, 0) else (0, 0)
            value = remains + pull if q == 0 else remains + added[key]
            total_ref[q, d, part, here, :] = value
            red = share * value
            if key != (0, 0):
                turn = turned[key[0], key[1], abs(c)]
                red = red + turn if sign > 0 else red - turn
            red_ref[q, d, part, here, :] = red

    def stream(row, d, parts):
        here = pl.ds(row, ROWS)
        totals, reds = [[], []], [[], []]
        for q in range(19):
            a, b, c = (int(v) for v in velocity_table[q])
            rows = pl.ds(row - a, ROWS)
            source = d if c == 0 else 1 - d
            if q:
                wall = [rock_ref[b + 1, source, part, rows, :] > 0.5 for part in range(parts)]
            for ref, found in ((total_ref, totals), (red_ref, reds)):
                if b == 0:
                    moved = [ref[q, source, part, rows, :] for part in range(parts)]
                else:
                    pair = [ref[q, source, part, rows, :] for part in range(2)]
                    edge = lane == (LANES - 1 if b > 0 else 0)
                    moved = [
                        pltpu.roll(jnp.where(edge, pair[1 - part], pair[part]), b % LANES, 1)
                        for part in range(parts)
                    ]
                for part in range(parts):
                    value = moved[part]
                    if q:
                        value = jnp.where(wall[part], ref[OPPOSITE[q], d, part, here, :], value)
                    found[part].append(value)
        return totals, reds

    def share_of(d, part, here, density_inverse, reds):
        rock = rock_ref[1, d, part, here, :] > 0.5
        return jnp.where(rock, label_ref[d, part, here, :], weighted_sum(reds) * density_inverse)

    def advance(row):
        here = pl.ds(row, ROWS)
        for d in range(2):
            totals, reds = stream(row, d, 2)
            for part in range(2):
                density, inverse, remains = relax(totals[part], rate)
                keep(d, part, here, density, share_of(d, part, here, inverse, reds[part]), remains)

    for number in range(ROUNDS):
        if number == 0:
            pack()
            pl.semaphore_wait(barrier, len(offsets))
        begin_round(number)
        for step in range(STEPS):
            low, high = 2 * step + 1, EXTENT - 2 * step - 1
            over_windows(low, high, collide)
            if step < STEPS - 1:
                over_windows(low + 1, high - 1, advance)
        if number < ROUNDS - 1:
            borders = [None] * (2 * (FIELDS - 1))
            for d in range(2):
                totals, reds = stream(HALO, d, 2)
                share = [
                    share_of(d, part, OWN, 1.0 / weighted_sum(totals[part]), reds[part]) for part in range(2)
                ]
                for q in range(19):
                    states[number + 1][q, d, OWN, :] = totals[0][q]
                    borders[2 * q + d] = totals[1][q]
                states[number + 1][19, d, OWN, :] = share[0]
                borders[2 * 19 + d] = share[1]
            pack_edges(borders)
        else:
            for d in range(2):
                totals, reds = stream(HALO, d, 1)
                rock = rock_ref[1, d, 0, OWN, :] > 0.5
                label = label_ref[d, 0, OWN, :]
                for q in range(19):
                    first = states[0][q, d, OWN, :]
                    out[0, q, d] = jnp.where(rock, first, totals[0][q])
                    out[1, q, d] = jnp.where(rock, label * first, reds[0][q])
    for copy in copies:
        copy.wait_send()


def body(populations, labels, solid, rates):
    in_place = pl.BlockSpec(memory_space=pl.ANY)
    field = (2, 2, EXTENT, LANES)
    return pl.pallas_call(
        kernel,
        out_shape=jax.ShapeDtypeStruct((2, 19, 2, ROWS, LANES), jnp.float32),
        in_specs=[in_place] * 4,
        out_specs=pl.BlockSpec(memory_space=pltpu.VMEM),
        scratch_shapes=[pltpu.VMEM((FIELDS, 2, EXTENT, LANES), jnp.float32)] * ROUNDS
        + [
            pltpu.VMEM((2, PACKED, EXTENT, LANES), jnp.float32),
            pltpu.VMEM((1, PACKED_LATER, EXTENT, LANES), jnp.float32),
            pltpu.VMEM((2, PACKED, ROWS, LANES), jnp.float32),
            pltpu.VMEM((2, 2, ROWS, LANES), jnp.int32),
            pltpu.SMEM((15,), jnp.float32),
            pltpu.VMEM((19,) + field, jnp.float32),
            pltpu.VMEM(field, jnp.float32),
            pltpu.VMEM(field, jnp.float32),
            pltpu.VMEM((19,) + field, jnp.float32),
            pltpu.VMEM((19,) + field, jnp.float32),
            pltpu.VMEM(field, jnp.float32),
            pltpu.VMEM((3,) + field, jnp.float32),
            pltpu.SemaphoreType.DMA((20,)),
            pltpu.SemaphoreType.DMA((20,)),
            pltpu.SemaphoreType.DMA((4,)),
        ],
        compiler_params=pltpu.CompilerParams(
            collective_id=0, has_side_effects=True, vmem_limit_bytes=32 * 2**20
        ),
    )(*[pltpu.with_memory_space_constraint(x, pltpu.HBM) for x in (rates, populations, labels, solid)])


def solution(mesh):
    return jax.shard_map(
        body,
        mesh=mesh,
        in_specs=(P(None, None, "gx", "gy"), P(None, "gx", "gy"), P(None, "gx", "gy"), P()),
        out_specs=P(None, None, None, "gx", "gy"),
        check_vma=False,
    )
```
